32 devices in a mesh: gx: 4 (over z), gy: 2 (over x), gz: 4 (over y, core).
Axes of the slice: x: 2, y: 2, z: 4, core: 2. Of those that a mesh axis runs over, the one named last changes fastest.
Arguments:
- fine_source_field: float32 [20, 20, 1280], P('gx', 'gy', 'gz'), may hold values from -6 to 6
- scaling: float32 [4, 4, 256], P('gx', 'gy', 'gz'), may hold values from 0.5 to 2
- block_fine: float32 [125, 125], replicated, may hold values from -5 to 16, as said below
- block_mid: float32 [27, 27], replicated, may hold values from -5 to 32, as said below
- block_coarse: float32 [8, 8], replicated, may hold values from -1 to 4, as said below
Outputs:
- solution: float32 [20, 20, 1280], P('gx', 'gy', 'gz')
The draws below stay inside these ranges and needn't reach their ends.
Inputs may be any that keep to these rules, and one draw needn't show every extreme that they name: `block_fine`: symmetric positive definite. `block_mid`: symmetric positive definite. `block_coarse`: symmetric positive definite.
All inputs are finite; a program needn't handle non-finite values.
Results may differ from the reference program's by a relative error of at most 0.0001.
Values sent between devices are 32-bit elements; how exact they have to be, the bound alone decides.
A program may use at most 64 MiB of HBM per device.

```python
import math
import jax
import jax.numpy as jnp
import numpy as np
from jax import lax

FINE_NODES_AXIS = 5
NM = 3
NC = 2
NU = 3
CSWEEPS = 4
ELEMENTS_X = 4
ELEMENTS_Y = 4
ELEMENTS_Z = 256


def gll_nodes(points):
    if points == 5:
        nodes = np.array([-1.0, -math.sqrt(3.0 / 7.0), 0.0, math.sqrt(3.0 / 7.0), 1.0])
        quadrature_weight = np.array([0.1, 49.0 / 90.0, 32.0 / 45.0, 49.0 / 90.0, 0.1])
        return (nodes, quadrature_weight)
    if points == 3:
        return (np.array([-1.0, 0.0, 1.0]), np.array([1.0 / 3.0, 4.0 / 3.0, 1.0 / 3.0]))
    return (np.array([-1.0, 1.0]), np.array([1.0, 1.0]))


def derivative(nodes):
    count = nodes.shape[0]
    table = np.zeros((count, count))
    for column in range(count):
        for other in range(count):
            if other != column:
                term = np.full(count, 1.0 / (nodes[column] - nodes[other]))
                for third in range(count):
                    if third != column and third != other:
                        term = term * (nodes - nodes[third]) / (nodes[column] - nodes[third])
                table[:, column] += term
    return table


def stiffness_tables(points):
    nodes, quadrature_weight = gll_nodes(points)
    slope = derivative(nodes)
    mass = np.eye(points) * quadrature_weight[None, :]
    line = np.dot(slope.T, np.dot(mass, slope))
    first = np.kron(np.kron(line, mass), mass)
    second = np.kron(np.kron(mass, line), mass)
    third = np.kron(np.kron(mass, mass), line)
    volume = np.kron(np.kron(quadrature_weight, quadrature_weight), quadrature_weight)
    return (first, second, third, volume)


def element_block(key, points):
    coef_key, shift_key, node_key = jax.random.split(key, 3)
    coefs = jnp.exp(jax.random.uniform(coef_key, (3,), jnp.float32, math.log(0.5), math.log(2.0)))
    shift = jnp.exp(jax.random.uniform(shift_key, (), jnp.float32, math.log(0.05), math.log(0.3)))
    rough = jax.random.uniform(node_key, (points ** 3,), jnp.float32, 0.5, 1.5)
    first, second, third, volume = stiffness_tables(points)
    block = coefs[0] * jnp.asarray(first, jnp.float32)
    block = block + coefs[1] * jnp.asarray(second, jnp.float32)
    block = block + coefs[2] * jnp.asarray(third, jnp.float32)
    added = shift * rough * jnp.asarray(volume, jnp.float32)
    return block + jnp.eye(points ** 3, dtype=jnp.float32) * added[None, :]


def draw_block_fine(key, part):
    key = jax.random.fold_in(key, 11)
    return element_block(key, FINE_NODES_AXIS)


def draw_block_mid(key, part):
    key = jax.random.fold_in(key, 23)
    return element_block(key, NM)


def draw_block_coarse(key, part):
    key = jax.random.fold_in(key, 37)
    return element_block(key, NC)


def level_of(stream_key, extent, cuts, low, top_value):
    gain, own = 1.0, jax.random.fold_in(stream_key, 6)
    for position, parts in cuts:
        heights = jnp.exp(jax.random.uniform(jax.random.fold_in(own, position), (parts,), jnp.float32, low / len(cuts), top_value / len(cuts)))
        gain = gain * jnp.repeat(heights, extent[position] // parts).reshape([-1 if axis == position else 1 for axis in range(len(extent))])
    return gain


def centred(stream_key, extent, width, most, cuts=(), held_as=jnp.bfloat16):
    values = jax.random.normal(stream_key, extent, jnp.float32) * width
    if len(cuts) > 0:
        values = level_of(stream_key, extent, cuts, -0.22, 0.18) * values
    return jnp.clip(values, min=-most, max=most).astype(held_as)


def setup_inputs(seed: int = 0) -> dict:
    key_of = jax.random.split(jax.random.key(seed), 6)
    fine_source_field = centred(key_of[0], (FINE_NODES_AXIS * ELEMENTS_X, FINE_NODES_AXIS * ELEMENTS_Y, FINE_NODES_AXIS * ELEMENTS_Z), 1.0, 6.0, ((0, 4), (1, 2), (2, 4)), jnp.float32)
    scaling = jnp.clip(jnp.exp(math.log(2.0) - 1.3862944 * jax.random.uniform(key_of[1], (ELEMENTS_X, ELEMENTS_Y, ELEMENTS_Z), jnp.float32) ** level_of(key_of[1], (ELEMENTS_X, ELEMENTS_Y, ELEMENTS_Z), ((0, 4), (1, 2), (2, 4)), -0.2, 0.2)), 0.5, 2.0)
    block_fine = draw_block_fine(jax.random.fold_in(key_of[5], 71), 0)
    block_mid = draw_block_mid(jax.random.fold_in(key_of[5], 71), 0)
    block_coarse = draw_block_coarse(jax.random.fold_in(key_of[5], 71), 0)
    return {"fine_source_field": fine_source_field, "scaling": scaling, "block_fine": block_fine, "block_mid": block_mid, "block_coarse": block_coarse}


penalty = 0.5
relax = 0.7

def gll_points(points):
    if points == 5:
        return np.array([-1.0, -math.sqrt(3.0 / 7.0), 0.0, math.sqrt(3.0 / 7.0), 1.0])
    if points == 3:
        return np.array([-1.0, 0.0, 1.0])
    return np.array([-1.0, 1.0])

def lagrange(fine_points, coarse_points):
    fine_nodes = gll_points(fine_points)
    coarse_nodes = gll_points(coarse_points)
    table = np.ones((fine_points, coarse_points))
    for column in range(coarse_points):
        for other in range(coarse_points):
            if other != column:
                table[:, column] *= (fine_nodes - coarse_nodes[other]) / (coarse_nodes[column] - coarse_nodes[other])
    return table

def along(values, table, dimension):
    out_points, in_points = table.shape
    moved = jnp.moveaxis(values, dimension, 0)
    elements = moved.shape[0] // in_points
    grouped = moved.reshape(elements, in_points, -1)
    mapped = jnp.einsum('oi,eir->eor', table, grouped, precision=lax.Precision.HIGHEST)
    mapped = mapped.reshape((elements * out_points,) + moved.shape[1:])
    return jnp.moveaxis(mapped, 0, dimension)

def prolong(values, fine_points, coarse_points):
    table = jnp.asarray(lagrange(fine_points, coarse_points), jnp.float32)
    for dimension in range(3):
        values = along(values, table, dimension)
    return values

def restrict(values, fine_points, coarse_points):
    table = jnp.asarray(lagrange(fine_points, coarse_points).T, jnp.float32)
    for dimension in range(3):
        values = along(values, table, dimension)
    return values

def expand(scaling, points):
    return jnp.repeat(jnp.repeat(jnp.repeat(scaling, points, 0), points, 1), points, 2)

def blocks(values, matrix, points):
    sizes = values.shape
    count_x, count_y, count_z = (sizes[0] // points, sizes[1] // points, sizes[2] // points)
    grid = values.reshape(count_x, points, count_y, points, count_z, points)
    grid = grid.transpose(1, 3, 5, 0, 2, 4).reshape(points ** 3, -1)
    result = jnp.dot(matrix.astype(jnp.float32), grid.astype(jnp.float32), precision=lax.Precision.HIGHEST, preferred_element_type=jnp.float32)
    result = result.reshape(points, points, points, count_x, count_y, count_z)
    return result.transpose(3, 0, 4, 1, 5, 2).reshape(sizes)

def neighbour(padded, sizes, dimension, offset):
    starts = [1, 1, 1]
    starts[dimension] = offset
    return lax.slice(padded, starts, [starts[place] + sizes[place] for place in range(3)])

def jumps(values, padded, points):
    total = jnp.zeros_like(values)
    for dimension in range(3):
        length = values.shape[dimension]
        local = jnp.arange(length) % points
        form = [1, 1, 1]
        form[dimension] = length
        first = (local == 0).astype(values.dtype).reshape(form)
        last = (local == points - 1).astype(values.dtype).reshape(form)
        before = neighbour(padded, values.shape, dimension, 0)
        after = neighbour(padded, values.shape, dimension, 2)
        total = total + first * (values - before) + last * (values - after)
    return total

def operate(values, scale, matrix, points, pad_fn):
    scaled = scale * values
    padded = pad_fn(scaled)
    return scale * (blocks(scaled, matrix, points) + penalty * jumps(scaled, padded, points))

def smoother_inverse(matrix, points):
    edge = ((jnp.arange(points) == 0) | (jnp.arange(points) == points - 1)).astype(matrix.dtype)
    counted = (edge[:, None, None] + edge[None, :, None] + edge[None, None, :]).reshape(points ** 3)
    identity_mat = jnp.eye(points ** 3, dtype=matrix.dtype)
    full = matrix + penalty * identity_mat * counted[None, :]
    lower = jnp.linalg.cholesky(full)
    half = lax.linalg.triangular_solve(lower, identity_mat, left_side=True, lower=True)
    return jnp.dot(half.T, half, precision=lax.Precision.HIGHEST)

def sweeps(guess, rhs, scale, matrix, inverse, points, count, pad_fn, cold):
    current = guess
    for step in range(count):
        if cold and step == 0:
            remainder = rhs
        else:
            remainder = rhs - operate(current, scale, matrix, points, pad_fn)
        current = current + relax * blocks(remainder, inverse, points) / (scale * scale)
    return current

def zero_pad(values):
    return jnp.pad(values, 1)

def reference(fine_source_field, scaling, block_fine, block_mid, block_coarse):
    scale_fine = expand(scaling, FINE_NODES_AXIS)
    scale_mid = expand(scaling, NM)
    scale_coarse = expand(scaling, NC)
    inverse_fine = smoother_inverse(block_fine, FINE_NODES_AXIS)
    inverse_mid = smoother_inverse(block_mid, NM)
    coarsest_inverse = smoother_inverse(block_coarse, NC)
    fine_iter = sweeps(jnp.zeros_like(fine_source_field), fine_source_field, scale_fine, block_fine, inverse_fine, FINE_NODES_AXIS, NU, zero_pad, True)
    fine_rest = fine_source_field - operate(fine_iter, scale_fine, block_fine, FINE_NODES_AXIS, zero_pad)
    mid_rhs = restrict(fine_rest, FINE_NODES_AXIS, NM)
    mid_iter = sweeps(jnp.zeros_like(mid_rhs), mid_rhs, scale_mid, block_mid, inverse_mid, NM, NU, zero_pad, True)
    mid_rest = mid_rhs - operate(mid_iter, scale_mid, block_mid, NM, zero_pad)
    coarse_rhs = restrict(mid_rest, NM, NC)
    coarse_iter = sweeps(jnp.zeros_like(coarse_rhs), coarse_rhs, scale_coarse, block_coarse, coarsest_inverse, NC, CSWEEPS, zero_pad, True)
    mid_iter = mid_iter + prolong(coarse_iter, NM, NC)
    mid_iter = sweeps(mid_iter, mid_rhs, scale_mid, block_mid, inverse_mid, NM, NU, zero_pad, False)
    fine_iter = fine_iter + prolong(mid_iter, FINE_NODES_AXIS, NM)
    return sweeps(fine_iter, fine_source_field, scale_fine, block_fine, inverse_fine, FINE_NODES_AXIS, NU, zero_pad, False)
```

```python
import functools
import math

import jax
import jax.numpy as jnp
import numpy as np
from jax import lax
from jax.experimental import pallas as pl
from jax.experimental.pallas import tpu as pltpu
from jax.sharding import PartitionSpec as P

FINE_NODES_AXIS = 5
NM = 3
NC = 2
NU = 3
CSWEEPS = 4


penalty = 0.5
relax = 0.7


def with_halo(cells, sides, width):
    for axis, dim in sides:
        count = lax.axis_size(axis)
        ends = count - 1
        head = lax.slice_in_dim(cells, 0, width, axis=dim)
        tail = lax.slice_in_dim(cells, cells.shape[dim] - width, cells.shape[dim], axis=dim)
        cells = jnp.concatenate(
            [
                lax.ppermute(tail, axis, [(i, (i + 1) % count) for i in range(ends)]),
                cells,
                lax.ppermute(head, axis, [((i + 1) % count, i) for i in range(ends)]),
            ],
            axis=dim,
        )
    return cells


def gll_points(points):
    if points == 5:
        return np.array([-1.0, -math.sqrt(3.0 / 7.0), 0.0, math.sqrt(3.0 / 7.0), 1.0])
    if points == 3:
        return np.array([-1.0, 0.0, 1.0])
    return np.array([-1.0, 1.0])


def lagrange(fine_points, coarse_points):
    fine_nodes = gll_points(fine_points)
    coarse_nodes = gll_points(coarse_points)
    table = np.ones((fine_points, coarse_points))
    for column in range(coarse_points):
        for other in range(coarse_points):
            if other != column:
                table[:, column] *= (fine_nodes - coarse_nodes[other]) / (
                    coarse_nodes[column] - coarse_nodes[other]
                )
    return table


def along(values, table, dimension):
    out_points, in_points = table.shape
    moved = jnp.moveaxis(values, dimension, 0)
    elements = moved.shape[0] // in_points
    grouped = moved.reshape(elements, in_points, -1)
    mapped = jnp.einsum("oi,eir->eor", table, grouped, precision=lax.Precision.HIGHEST)
    mapped = mapped.reshape((elements * out_points,) + moved.shape[1:])
    return jnp.moveaxis(mapped, 0, dimension)


def prolong(values, fine_points, coarse_points):
    table = jnp.asarray(lagrange(fine_points, coarse_points), jnp.float32)
    for dimension in range(3):
        values = along(values, table, dimension)
    return values


def restrict(values, fine_points, coarse_points):
    table = jnp.asarray(lagrange(fine_points, coarse_points).T, jnp.float32)
    for dimension in range(3):
        values = along(values, table, dimension)
    return values


def expand(scaling, points):
    return jnp.repeat(jnp.repeat(jnp.repeat(scaling, points, 0), points, 1), points, 2)


def blocks(values, matrix, points):
    sizes = values.shape
    count_x, count_y, count_z = (sizes[0] // points, sizes[1] // points, sizes[2] // points)
    grid = values.reshape(count_x, points, count_y, points, count_z, points)
    grid = grid.transpose(1, 3, 5, 0, 2, 4).reshape(points**3, -1)
    result = jnp.dot(
        matrix, grid, precision=lax.Precision.HIGHEST, preferred_element_type=jnp.float32
    )
    result = result.reshape(points, points, points, count_x, count_y, count_z)
    return result.transpose(3, 0, 4, 1, 5, 2).reshape(sizes)


def neighbour(padded, sizes, dimension, offset):
    starts = [1, 1, 1]
    starts[dimension] = offset
    return lax.slice(padded, starts, [starts[place] + sizes[place] for place in range(3)])


def jumps(values, padded, points):
    total = jnp.zeros_like(values)
    for dimension in range(3):
        length = values.shape[dimension]
        local = jnp.arange(length) % points
        form = [1, 1, 1]
        form[dimension] = length
        first = (local == 0).astype(values.dtype).reshape(form)
        last = (local == points - 1).astype(values.dtype).reshape(form)
        before = neighbour(padded, values.shape, dimension, 0)
        after = neighbour(padded, values.shape, dimension, 2)
        total = total + first * (values - before) + last * (values - after)
    return total


def operate(values, scale, matrix, points, pad_fn):
    scaled = scale * values
    padded = pad_fn(scaled)
    return scale * (blocks(scaled, matrix, points) + penalty * jumps(scaled, padded, points))


def smoother_inverse(matrix, points):
    edge = ((jnp.arange(points) == 0) | (jnp.arange(points) == points - 1)).astype(matrix.dtype)
    counted = (edge[:, None, None] + edge[None, :, None] + edge[None, None, :]).reshape(points**3)
    identity_mat = jnp.eye(points**3, dtype=matrix.dtype)
    full = matrix + penalty * identity_mat * counted[None, :]
    lower = jnp.linalg.cholesky(full)
    half = lax.linalg.triangular_solve(lower, identity_mat, left_side=True, lower=True)
    return jnp.dot(half.T, half, precision=lax.Precision.HIGHEST)


def sweeps(guess, rhs, scale, matrix, inverse, points, count, pad_fn, cold):
    current = guess
    for step in range(count):
        if cold and step == 0:
            remainder = rhs
        else:
            remainder = rhs - operate(current, scale, matrix, points, pad_fn)
        current = current + relax * blocks(remainder, inverse, points) / (scale * scale)
    return current


def pad_grid(values):
    return with_halo(values, (("gx", 0), ("gy", 1), ("gz", 2)), 1)


def per_device(fine_source_field, scaling, block_fine, block_mid, block_coarse):
    scale_fine = expand(scaling, FINE_NODES_AXIS)
    scale_mid = expand(scaling, NM)
    inverse_fine = smoother_inverse(block_fine, FINE_NODES_AXIS)
    inverse_mid = smoother_inverse(block_mid, NM)
    coarsest_inverse = smoother_inverse(block_coarse, NC)
    fine_iter = sweeps(
        jnp.zeros_like(fine_source_field),
        fine_source_field,
        scale_fine,
        block_fine,
        inverse_fine,
        FINE_NODES_AXIS,
        NU,
        pad_grid,
        True,
    )
    fine_rest = fine_source_field - operate(
        fine_iter, scale_fine, block_fine, FINE_NODES_AXIS, pad_grid
    )
    mid_rhs = restrict(fine_rest, FINE_NODES_AXIS, NM)
    mid_iter = sweeps(
        jnp.zeros_like(mid_rhs), mid_rhs, scale_mid, block_mid, inverse_mid, NM, NU, pad_grid, True
    )
    mid_rest = mid_rhs - operate(mid_iter, scale_mid, block_mid, NM, pad_grid)
    coarse_rhs = restrict(mid_rest, NM, NC)
    scale_coarse = expand(scaling, NC)
    coarse_iter = sweeps(
        jnp.zeros_like(coarse_rhs),
        coarse_rhs,
        scale_coarse,
        block_coarse,
        coarsest_inverse,
        NC,
        CSWEEPS,
        pad_grid,
        True,
    )
    mid_iter = mid_iter + prolong(coarse_iter, NM, NC)
    mid_iter = sweeps(mid_iter, mid_rhs, scale_mid, block_mid, inverse_mid, NM, NU, pad_grid, False)
    fine_iter = fine_iter + prolong(mid_iter, FINE_NODES_AXIS, NM)
    return sweeps(
        fine_iter,
        fine_source_field,
        scale_fine,
        block_fine,
        inverse_fine,
        FINE_NODES_AXIS,
        NU,
        pad_grid,
        False,
    )


HALO = 16
MESH = pl.DeviceIdType.MESH
HIGHEST = lax.Precision.HIGHEST


def trace_tables(points, width, lanes):
    take = np.zeros((128, lanes), np.float32)
    put = np.zeros((lanes, 128), np.float32)
    for dim in range(3):
        for side in range(2):
            slot = 2 * dim + side
            for u in range(points):
                for v in range(points):
                    out_index, in_index = [u, v], [u, v]
                    out_index.insert(dim, points - 1 if side == 0 else 0)
                    in_index.insert(dim, 0 if side == 0 else points - 1)
                    flat_out = (out_index[0] * points + out_index[1]) * points + out_index[2]
                    flat_in = (in_index[0] * points + in_index[1]) * points + in_index[2]
                    lane = slot * width + u * points + v
                    take[flat_out, lane] = 1.0
                    put[lane, flat_in] = 1.0
    return take, put


def edge_count(points):
    edge = np.zeros(points, np.float32)
    edge[0] = edge[-1] = 1.0
    count = edge[:, None, None] + edge[None, :, None] + edge[None, None, :]
    return count.reshape(-1)


def padded(table, rows, columns):
    full = np.zeros((rows, columns), np.float32)
    full[: table.shape[0], : table.shape[1]] = table
    return full


def cube(table):
    return np.kron(np.kron(table, table), table)


def split(x):
    high = x.astype(jnp.bfloat16)
    return high, (x - high.astype(jnp.float32)).astype(jnp.bfloat16)


def mm(x, pair):
    high, low = split(x)
    dot = functools.partial(jnp.dot, preferred_element_type=jnp.float32)
    return dot(high, pair[0]) + (dot(high, pair[1]) + dot(low, pair[0]))


def invert(rows, size, panel):
    lanes = lax.broadcasted_iota(jnp.int32, (8, 128), 1)
    subs = lax.broadcasted_iota(jnp.int32, (8, 128), 0)
    for start in range(0, size, panel):
        pivots = list(range(start, min(start + panel, size)))
        columns = {k: [jnp.broadcast_to(r[:, k : k + 1], (8, 128)) for r in rows] for k in pivots}
        for k in pivots:
            block, sub = k // 8, k % 8
            column = columns[k]
            inverse = 1.0 / column[block][sub : sub + 1, :]
            here = lanes[:1] == k
            scaled = jnp.where(here, 1.0, rows[block][sub : sub + 1, :]) * inverse
            mine = subs == sub
            rows = [jnp.where(lanes == k, 0.0, r) - c * scaled for r, c in zip(rows, column)]
            rows[block] = jnp.where(mine, scaled, rows[block])
            for later in pivots:
                if later > k:
                    factor = columns[later][block][sub : sub + 1, :] * inverse
                    fresh = [d - c * factor for d, c in zip(columns[later], column)]
                    fresh[block] = jnp.where(mine, factor, fresh[block])
                    columns[later] = fresh
    return jnp.concatenate(rows, axis=0)


def prepared(block_ref, frame, points, panel, count_ref):
    size = points**3
    blocks8 = -(-size // 8)
    frame[...] = count_ref[...]
    frame[0:size, 0:size] = frame[0:size, 0:size] + block_ref[...]
    rows = [frame[8 * n : 8 * n + 8, :] for n in range(blocks8)]
    inverse = invert(rows, size, panel)
    if blocks8 < 16:
        inverse = jnp.concatenate(
            [inverse, jnp.zeros((128 - 8 * blocks8, 128), jnp.float32)], axis=0
        )
    return inverse


def cycle_kernel(shape, z_first, cells_ref, bf_ref, bm_ref, bc_ref, *refs):
    (cf, cm, cc, take_f, put_f, take_m, put_m, take_c, put_c, k1, pk1, kt1, kte1, k2, pk2, kt2, kte2) = refs[:17]
    out_ref, frame_f, frame_m, frame_c = refs[17:]
    nx, ny, depth, own, z_count = shape
    rows = nx * ny * depth
    exact = functools.partial(jnp.dot, precision=HIGHEST, preferred_element_type=jnp.float32)

    def derived(inverse, take, put):
        lift = exact((0.5 * relax) * put[...], inverse)
        sweep = exact(lift, take[...])
        return split(relax * inverse), split(relax * exact(inverse, take[...])), split(lift), split(sweep)

    g_f, ge_f, lift_f, w_f = derived(prepared(bf_ref, frame_f, FINE_NODES_AXIS, 5, cf), take_f, put_f)
    g_m, ge_m, lift_m, w_m = derived(prepared(bm_ref, frame_m, NM, 3, cm), take_m, put_m)
    g_c, ge_c, lift_c, w_c = derived(prepared(bc_ref, frame_c, NC, 4, cc), take_c, put_c)

    z = z_first() + lax.rem(lax.broadcasted_iota(jnp.int32, (rows, 128), 0), depth)
    lane = lax.broadcasted_iota(jnp.int32, (rows, 128), 1)
    has_before = (z >= 1) & (z <= z_count)
    has_after = (z >= -1) & (z <= z_count - 2)
    inside = (z >= 0) & (z < z_count)

    def shifted(t, slot):
        if slot >= 4:
            if slot == 4:
                return jnp.where(has_before, pltpu.roll(t, 1, 0), 0.0)
            return jnp.where(has_after, pltpu.roll(t, rows - 1, 0), 0.0)
        if slot < 2:
            step = ny * depth
            zero = jnp.zeros((step, 128), jnp.float32)
            if slot == 0:
                return jnp.concatenate([zero, t[: rows - step]], axis=0)
            return jnp.concatenate([t[step:], zero], axis=0)
        zero = jnp.zeros((depth, 128), jnp.float32)
        parts = []
        for a in range(nx):
            low, high = a * ny * depth, (a + 1) * ny * depth
            if slot == 2:
                parts += [zero, t[low : high - depth]]
            else:
                parts += [t[low + depth : high], zero]
        return jnp.concatenate(parts, axis=0)

    def arrive_small(t):
        out = shifted(t, 5)
        for slot in range(4, -1, -1):
            out = jnp.where(lane < 16 * (slot + 1), shifted(t, slot), out)
        return out

    def arrive_fine(t):
        first, second = t[:, :128], t[:, 128:]
        out = shifted(first, 3)
        for slot in range(2, -1, -1):
            out = jnp.where(lane < 32 * (slot + 1), shifted(first, slot), out)
        last = jnp.where(lane < 32, shifted(second, 4), shifted(second, 5))
        return jnp.concatenate([out, last], axis=1)

    keep = 1.0 - relax

    def cold(tc, arrive, w):
        r1 = arrive(tc)
        t2 = (1.0 + keep) * tc + mm(r1, w)
        r2 = arrive(t2)
        t3 = keep * t2 + tc + mm(r2, w)
        gathered = r2 + keep * r1
        rest = 0.5 * arrive(t3) - (0.5 * relax) * gathered
        return t3, gathered, rest

    def warm(t, tc, arrive, w):
        r0 = arrive(t)
        t1 = keep * t + tc + mm(r0, w)
        r1 = arrive(t1)
        t2 = keep * t1 + tc + mm(r1, w)
        return arrive(t2) + keep * r1 + (keep * keep) * r0

    full = 1.0 + keep + keep * keep
    cube_keep = keep**3
    cells = cells_ref[...].reshape(rows, 128)
    scale = jnp.where(inside, jnp.broadcast_to(cells[:, 125:126], (rows, 128)), 1.0)
    unscale = 1.0 / scale
    source = cells * unscale

    tc_f = mm(source, ge_f)
    t3_f, got_f, rest_f = cold(tc_f, arrive_fine, w_f)
    rhs_m = cube_keep * mm(cells, split(k1[...])) + scale * mm(rest_f, split(pk1[...]))

    source_m = rhs_m * unscale
    c_m = mm(source_m, g_m)
    tc_m = mm(source_m, ge_m)
    t3_m, got_m, rest_m = cold(tc_m, arrive_small, w_m)
    rhs_c = cube_keep * mm(rhs_m, split(k2[...])) + scale * mm(rest_m, split(pk2[...]))

    source_c = rhs_c * unscale
    c_c = mm(source_c, g_c)
    tc_c = mm(source_c, ge_c)
    r = arrive_small(tc_c)
    gathered = r
    t = (1.0 + keep) * tc_c + mm(r, w_c)
    for _ in range(CSWEEPS - 3):
        r = arrive_small(t)
        gathered = r + keep * gathered
        t = keep * t + tc_c + mm(r, w_c)
    gathered = arrive_small(t) + keep * gathered
    y_c = sum(keep**n for n in range(CSWEEPS)) * c_c + mm(gathered, lift_c)

    t_m = t3_m + mm(y_c, split(kte2[...]))
    base_m = full * c_m + mm(y_c, split(cube_keep * kt2[...]))
    got = warm(t_m, tc_m, arrive_small, w_m) + cube_keep * got_m
    y_m = base_m + (cube_keep * full) * c_m + mm(got, lift_m)

    t_f = t3_f + mm(y_m, split(kte1[...]))
    got = warm(t_f, tc_f, arrive_fine, w_f) + cube_keep * got_f

    def owned(x):
        return jnp.concatenate(
            [x[n * depth + HALO : n * depth + HALO + own] for n in range(nx * ny)], axis=0
        )

    y_f = (
        (full + cube_keep * full) * mm(owned(source), g_f)
        + mm(owned(y_m), split(cube_keep * kt1[...]))
        + mm(owned(got), lift_f)
    )
    out_ref[...] = (y_f * owned(unscale)).reshape(out_ref.shape)


def windows(group, slab, z_local):
    found = []
    for rank in range(group):
        for step in (-1, 0, 1):
            first = slab * rank - HALO + step * z_local
            low, high = max(0, first), min(z_local, first + slab + 2 * HALO)
            if low < high:
                found.append((rank, step, low, high - low, low - first))
    return found


def gather_kernel(counts, slab, z_local, src, dst, send_sem, recv_sem, own_sem):
    gx, gy, gz = counts
    group = gx * gy
    x, y, g = lax.axis_index("gx"), lax.axis_index("gy"), lax.axis_index("gz")
    rank = x * gy + y
    plan = windows(group, slab, z_local)

    def peer(number, step):
        return (number // gy, number % gy, lax.rem(g + step + gz, gz))

    barrier = pltpu.get_barrier_semaphore()
    for target in range(group):

        @pl.when(rank == target)
        def _():
            for entry in plan:
                for other in range(group):
                    if entry[0] == target and not (entry[1] == 0 and other == target):
                        pl.semaphore_signal(
                            barrier, inc=1, device_id=peer(other, -entry[1]), device_id_type=MESH
                        )

    pl.semaphore_wait(barrier, len(plan) - 1)

    def copy(n, entry):
        target, step, low, size, place = entry
        return pltpu.make_async_remote_copy(
            src_ref=src.at[:, pl.ds(low, size)],
            dst_ref=dst.at[x, y, :, pl.ds(place, size)],
            send_sem=send_sem.at[n],
            recv_sem=recv_sem.at[(step + 1) * group + rank],
            device_id=peer(target, step),
            device_id_type=MESH,
        )

    def local(entry):
        _, _, low, size, place = entry
        return pltpu.make_async_copy(
            src.at[:, pl.ds(low, size)], dst.at[x, y, :, pl.ds(place, size)], own_sem.at[0]
        )

    for n, entry in enumerate(plan):
        if entry[1] != 0:
            copy(n, entry).start()
            continue

        @pl.when(rank != entry[0])
        def _():
            copy(n, entry).start()

        @pl.when(rank == entry[0])
        def _():
            local(entry).start()

    for n, entry in enumerate(plan):
        if entry[1] != 0:
            copy(n, entry).wait_send()
            continue

        @pl.when(rank != entry[0])
        def _():
            copy(n, entry).wait_send()

    def arrived(entry, other):
        _, step, low, size, place = entry
        return pltpu.make_async_remote_copy(
            src_ref=src.at[:, pl.ds(low, size)],
            dst_ref=dst.at[other // gy, other % gy, :, pl.ds(place, size)],
            send_sem=send_sem.at[0],
            recv_sem=recv_sem.at[(step + 1) * group + other],
            device_id=peer(other, -step),
            device_id_type=MESH,
        )

    for target in range(group):

        @pl.when(rank == target)
        def _():
            for entry in plan:
                for other in range(group):
                    if entry[0] == target:
                        if entry[1] == 0 and other == target:
                            local(entry).wait()
                        else:
                            arrived(entry, other).wait_recv()


def scatter_kernel(counts, slab, src, dst, send_sem, recv_sem, own_sem):
    gx, gy, _ = counts
    group = gx * gy
    x, y, g = lax.axis_index("gx"), lax.axis_index("gy"), lax.axis_index("gz")
    rank = x * gy + y
    barrier = pltpu.get_barrier_semaphore()
    others = []
    for step in range(1, group):
        number = lax.rem(rank + step, group)
        others.append((number // gy, number % gy, g))
    for other in others:
        pl.semaphore_signal(barrier, inc=1, device_id=other, device_id_type=MESH)
    pl.semaphore_wait(barrier, group - 1)
    place = pl.ds(pl.multiple_of(rank * slab, 8), slab)
    copies = []
    for n, other in enumerate(others):
        copies.append(
            pltpu.make_async_remote_copy(
                src_ref=src.at[other[0], other[1]],
                dst_ref=dst.at[:, place],
                send_sem=send_sem.at[n],
                recv_sem=recv_sem.at[n],
                device_id=other,
                device_id_type=MESH,
            )
        )
        copies[-1].start()
    mine = pltpu.make_async_copy(src.at[x, y], dst.at[:, place], own_sem.at[0])
    mine.start()
    for one in copies:
        one.wait_send()
    for one in copies:
        one.wait_recv()
    mine.wait()


def tables():
    out = []
    for points in (FINE_NODES_AXIS, NM, NC):
        diagonal = np.ones(128, np.float32)
        diagonal[: points**3] = penalty * edge_count(points)
        out.append(np.diag(diagonal))
    fine = trace_tables(FINE_NODES_AXIS, 32, 256)
    middle = trace_tables(NM, 16, 128)
    coarse = trace_tables(NC, 16, 128)
    out += [*fine, *middle, *coarse]
    for (take, put), high, low in ((fine, FINE_NODES_AXIS, NM), (middle, NM, NC)):
        down = padded(cube(lagrange(high, low)), 128, 128)
        out += [down, put @ down, down.T, down.T @ take]
    return [jnp.asarray(table, jnp.float32) for table in out]


def slab_device(counts, fine_source_field, scaling, block_fine, block_mid, block_coarse):
    gx, gy, gz = counts
    ex, ey, ez = scaling.shape
    p = FINE_NODES_AXIS
    group = gx * gy
    slab = ez // group
    depth = slab + 2 * HALO
    cells = fine_source_field.reshape(ex, p, ey, p, ez, p).transpose(0, 2, 4, 1, 3, 5)
    cells = cells.reshape(ex * ey, ez, p**3)
    scales = scaling.reshape(ex * ey, ez, 1)
    packed = jnp.concatenate(
        [cells, scales, jnp.zeros((ex * ey, ez, 128 - p**3 - 1), jnp.float32)], axis=2
    )
    vmem = pl.BlockSpec(memory_space=pltpu.VMEM)
    steps = len(windows(group, slab, ez))
    gathered = pl.pallas_call(
        functools.partial(gather_kernel, counts, slab, ez),
        out_shape=jax.ShapeDtypeStruct((gx, gy, ex * ey, depth, 128), jnp.float32),
        in_specs=[vmem],
        out_specs=vmem,
        scratch_shapes=[
            pltpu.SemaphoreType.DMA((steps,)),
            pltpu.SemaphoreType.DMA((3 * group,)),
            pltpu.SemaphoreType.DMA((1,)),
        ],
        compiler_params=pltpu.CompilerParams(collective_id=0, has_side_effects=True),
        name="gather_slab",
    )(packed)

    def z_first():
        rank = lax.axis_index("gx") * gy + lax.axis_index("gy")
        return lax.axis_index("gz") * ez + rank * slab - HALO

    constants = tables()
    shape = (gx * ex, gy * ey, depth, slab, gz * ez)
    result = pl.pallas_call(
        functools.partial(cycle_kernel, shape, z_first),
        out_shape=jax.ShapeDtypeStruct((gx, gy, ex * ey, slab, 128), jnp.float32),
        in_specs=[vmem] * (4 + len(constants)),
        out_specs=vmem,
        scratch_shapes=[pltpu.VMEM((128, 128), jnp.float32)] * 3,
        compiler_params=pltpu.CompilerParams(vmem_limit_bytes=40 * 1024 * 1024),
        name="v_cycle",
    )(gathered, block_fine, block_mid, block_coarse, *constants)
    back = pl.pallas_call(
        functools.partial(scatter_kernel, counts, slab),
        out_shape=jax.ShapeDtypeStruct((ex * ey, ez, 128), jnp.float32),
        in_specs=[vmem],
        out_specs=vmem,
        scratch_shapes=[
            pltpu.SemaphoreType.DMA((group - 1,)),
            pltpu.SemaphoreType.DMA((group - 1,)),
            pltpu.SemaphoreType.DMA((1,)),
        ],
        compiler_params=pltpu.CompilerParams(collective_id=1, has_side_effects=True),
        name="scatter_slab",
    )(result)
    cells = back[:, :, : p**3].reshape(ex, ey, ez, p, p, p).transpose(0, 3, 1, 4, 2, 5)
    return cells.reshape(fine_source_field.shape)


def solution(mesh):
    in_specs = (P("gx", "gy", "gz"), P("gx", "gy", "gz"), P(), P(), P())
    out_specs = P("gx", "gy", "gz")
    counts = tuple(mesh.shape[axis] for axis in ("gx", "gy", "gz"))

    def body(fine_source_field, scaling, *matrices):
        ex, _, ez = scaling.shape
        group = counts[0] * counts[1]
        if ex == 1 and ez % (8 * group) == 0 and ez >= HALO and counts[2] >= 3:
            return slab_device(counts, fine_source_field, scaling, *matrices)
        return per_device(fine_source_field, scaling, *matrices)

    return jax.shard_map(
        body, mesh=mesh, in_specs=in_specs, out_specs=out_specs, check_vma=False
    )
```
